512 devices in a mesh: seq: 128 (over y, z, core), head: 4 (over x).
Axes of the slice: x: 4, y: 4, z: 16, core: 2. Of those that a mesh axis runs over, the one named last changes fastest.
Arguments:
- queries: bfloat16 [32768, 2048], P('seq', 'head'), may hold values from -6 to 6
- keys: bfloat16 [32768, 2048], P('seq', 'head'), may hold values from -40 to 40
- values: bfloat16 [32768, 2048], P('seq', 'head'), may hold values from -24 to 24
- ridges: float32 [16], P('head'), may hold values from 0.25 to 4
- out_weight: bfloat16 [2048, 2048], P('head'), may hold values from -0.125 to 0.125
Outputs:
- layer_out: bfloat16 [32768, 2048], P('seq', 'head')
The draws below stay inside these ranges and needn't reach their ends.
All inputs are finite; a program needn't handle non-finite values.
Results may differ from the reference program's by a relative error of at most 0.0049.
Values may be sent and summed in bfloat16 or wider, within the bound.
No kernel may reach another device: no remote copies, remote signals or barrier semaphores. Data moves between devices by JAX's collectives and lax.ppermute only.
A program may use at most 128 MiB of HBM per device.

```python
import math
import jax
import jax.numpy as jnp
from jax import lax

D = 2048
HEADS = 16
HD = 128
SPAN = 128
ITERS = 2
TOKENS = 32768


def draw_keys(key, part):
    first, second = jax.random.split(key, 2)
    scales = jnp.exp(jax.random.uniform(first, (1, HEADS * HD), jnp.float32, 0.0, math.log(10.0)))
    base = jax.random.normal(second, (TOKENS, HEADS * HD), jnp.float32) * scales
    return jnp.clip(base, -40.0, 40.0).astype(jnp.bfloat16)


def levels(own_key, dims, pieces, smallest, largest):
    loudness, own = 1.0, jax.random.fold_in(own_key, 6)
    for axis_at, shards_of in pieces:
        steps = jnp.exp(jax.random.uniform(jax.random.fold_in(own, axis_at), (shards_of,), jnp.float32, smallest / len(pieces), largest / len(pieces)))
        loudness = loudness * jnp.repeat(steps, dims[axis_at] // shards_of).reshape([-1 if axis == axis_at else 1 for axis in range(len(dims))])
    return loudness


def noise(stream_key, dims, width, most, cuts=(), held_as=jnp.bfloat16):
    level = levels(stream_key, dims, cuts, -0.22, 0.18) if cuts else 1.0
    values = jax.random.normal(stream_key, dims, jnp.float32) * width * level
    return jnp.minimum(jnp.maximum(values, -most), most).astype(held_as)


def setup_inputs(seed: int = 0) -> dict:
    arg_keys = jax.random.split(jax.random.key(seed), 6)
    queries = noise(arg_keys[0], (TOKENS, HEADS * HD), 1.0, 6.0, ((0, 128), (1, 4)))
    keys = draw_keys(jax.random.fold_in(arg_keys[5], 71), 0)
    values = noise(arg_keys[2], (TOKENS, HEADS * HD), 4.0, 24.0, ((0, 128), (1, 4)))
    ridges = jnp.clip(jnp.exp(math.log(4.0) - 2.7725887 * jax.random.uniform(arg_keys[3], (HEADS,), jnp.float32) ** levels(arg_keys[3], (HEADS,), ((0, 4),), -0.2, 0.2)), 0.25, 4.0)
    out_weight = noise(arg_keys[4], (HEADS * HD, D), (HEADS * HD) ** -0.5, 0.125, ((0, 4),))
    return dict(queries=queries, keys=keys, values=values, ridges=ridges, out_weight=out_weight)


highest = lax.Precision.HIGHEST

def normalize(entries):
    return entries * lax.rsqrt(lax.optimization_barrier(jnp.sum(entries * entries, axis=-1, keepdims=True)) + 1e-06)

def product(left, right):
    return jnp.dot(left, right, precision=highest, preferred_element_type=jnp.float32)

def solve_block(queries_b, keyrows, values_b, key_state, value_state, ridge_value):
    block_len = queries_b.shape[0]
    causal = (lax.broadcasted_iota(jnp.int32, (block_len, block_len), 0) >= lax.broadcasted_iota(jnp.int32, (block_len, block_len), 1)).astype(jnp.float32)

    def within(inputs, payload):
        scores = product(inputs, keyrows.T) * causal
        return product(scores, payload)

    def operate(direction):
        return ridge_value * direction + within(direction, keyrows) + product(direction, key_state)
    estimate = jnp.zeros_like(queries_b)
    residual = queries_b
    direction = queries_b
    res_norm = lax.optimization_barrier(jnp.sum(residual * residual, axis=-1, keepdims=True))
    for sweep in range(ITERS):
        applied = operate(direction)
        step_size = res_norm / (lax.optimization_barrier(jnp.sum(direction * applied, axis=-1, keepdims=True)) + 1e-06)
        estimate = estimate + step_size * direction
        residual = residual - step_size * applied
        fresh = lax.optimization_barrier(jnp.sum(residual * residual, axis=-1, keepdims=True))
        direction = residual + fresh / (res_norm + 1e-06) * direction
        res_norm = fresh
    return product(estimate, value_state) + within(estimate, values_b)

def one_head(operands):
    head_q, head_k, head_v, ridge_value = operands
    blocks_q = normalize(head_q).reshape(-1, SPAN, HD)
    blocks_k = normalize(head_k).reshape(-1, SPAN, HD)
    blocks_v = head_v.reshape(-1, SPAN, HD)

    def advance(carry, block):
        key_state, value_state = carry
        block_q, block_k, block_v = block
        result = solve_block(block_q, block_k, block_v, key_state, value_state, ridge_value)
        key_state = key_state + product(block_k.T, block_k)
        value_state = value_state + product(block_k.T, block_v)
        return ((key_state, value_state), result)
    start = (jnp.zeros((HD, HD), jnp.float32), jnp.zeros((HD, HD), jnp.float32))
    unused, results = lax.scan(advance, start, (blocks_q, blocks_k, blocks_v))
    return results.reshape(TOKENS, HD)

def reference(queries, keys, values, ridges, out_weight):
    split_q = queries.astype(jnp.float32).reshape(TOKENS, HEADS, HD).transpose(1, 0, 2)
    split_k = keys.astype(jnp.float32).reshape(TOKENS, HEADS, HD).transpose(1, 0, 2)
    split_v = values.astype(jnp.float32).reshape(TOKENS, HEADS, HD).transpose(1, 0, 2)
    outputs = lax.map(one_head, (split_q, split_k, split_v, ridges.astype(jnp.float32)))
    mixed = outputs.transpose(1, 0, 2).reshape(TOKENS, HEADS * HD).astype(jnp.bfloat16)
    return jnp.dot(mixed, out_weight, preferred_element_type=jnp.float32).astype(jnp.bfloat16)
```

```python
import jax
import jax.numpy as jnp
from jax import lax
from jax.experimental import pallas as pl
from jax.experimental.pallas import tpu as pltpu
from jax.sharding import Mesh
from jax.sharding import PartitionSpec as P

HD = 128
ITERS = 2
SEQ = ("y", "far", "near", "core")
NEAR = ("y", "near", "core")
EPS = 1e-06
f32, bf16 = jnp.float32, jnp.bfloat16


def vmem():
    return pl.BlockSpec(memory_space=pltpu.VMEM)


def smem():
    return pl.BlockSpec(memory_space=pltpu.SMEM)


def params():
    return pltpu.CompilerParams(vmem_limit_bytes=32 * 1024 * 1024)


def halves(value):
    high = value.astype(bf16)
    return high, (value - high.astype(f32)).astype(bf16)


def pack(value):
    return (value * value * (value * jnp.abs(value))).astype(bf16)


def unpack(coded):
    coded = coded.astype(f32)
    root = jnp.sqrt(jnp.sqrt(jnp.abs(coded)))
    return jnp.where(coded < 0.0, -root, root)


def stacked(value):
    return jnp.concatenate(halves(value), axis=0)


def dot(left, right):
    return jnp.dot(left, right, preferred_element_type=f32)


def key_scale(keys):
    keys = keys.astype(f32)
    return lax.rsqrt(jnp.sum(keys * keys, axis=1, keepdims=True) + EPS)


def grams(k_ref, v_ref, out_ref):
    heads = k_ref.shape[1] // HD
    for h in range(heads):
        cols = slice(h * HD, (h + 1) * HD)
        keys, values = k_ref[:, cols], v_ref[:, cols]
        scale = key_scale(keys)
        kn = keys.astype(f32) * scale
        key_side = jnp.concatenate(halves(kn * scale), axis=1)
        value_side = jnp.concatenate(halves(kn), axis=1)
        key_gram = dot(keys.T, key_side)
        value_gram = dot(values.T, value_side)
        out_ref[h] = pack(key_gram[:, :HD] + key_gram[:, HD:])
        out_ref[heads + h] = pack(value_gram[:, :HD] + value_gram[:, HD:])


def group_totals(near_ref, out_ref):
    for y in range(near_ref.shape[0]):
        total = unpack(near_ref[y, 0])
        for member in range(1, near_ref.shape[1]):
            total += unpack(near_ref[y, member])
        total = pack(total)
        for far in range(out_ref.shape[0]):
            out_ref[far, y] = total


def prefixes(mine_ref, near_ref, far_ref, out_ref):
    mine = mine_ref[0]
    before = jnp.zeros(near_ref.shape[2:], f32)
    for y in range(near_ref.shape[0]):
        running = before
        for far in range(far_ref.shape[0]):
            total = unpack(far_ref[far, y])
            running += jnp.where(far < mine, total, 0.0)
            before += total
        for member in range(near_ref.shape[1]):
            out_ref[y, member] = pack(running)
            running += unpack(near_ref[y, member])


def solve(ridge_ref, q_ref, k_ref, v_ref, state_ref, w_ref, out_ref, mixed_ref):
    tokens, width = q_ref.shape
    heads = width // HD
    causal = lax.broadcasted_iota(jnp.int32, (tokens, tokens), 0) <= lax.broadcasted_iota(
        jnp.int32, (tokens, tokens), 1
    )
    for h in range(heads):
        cols = slice(h * HD, (h + 1) * HD)
        keys, values = k_ref[:, cols], v_ref[:, cols]
        scale = key_scale(keys)
        weight_k = jnp.where(causal, scale * scale, 0.0)
        weight_v = jnp.where(causal, scale, 0.0)
        keys_t = keys.T
        key_state = halves(unpack(state_ref[h]))
        value_state = halves(unpack(state_ref[heads + h]))

        def apply(state, split, weight, payload):
            left = jnp.concatenate([keys, state[0]], axis=0)
            both = dot(jnp.concatenate([left] * (split.shape[0] // HD), axis=1), split)
            scores = stacked(both[:tokens] * weight)
            within = dot(jnp.concatenate([payload, payload], axis=1), scores)
            return both[tokens:] + dot(state[1], split[:HD]) + within

        raw = q_ref[:, cols].T
        raw_f = raw.astype(f32)
        q_scale = lax.rsqrt(jnp.sum(raw_f * raw_f, axis=0, keepdims=True) + EPS)
        residual = raw_f * q_scale
        direction = residual
        norm = jnp.sum(residual * residual, axis=0, keepdims=True)
        estimate = None
        for sweep in range(ITERS):
            if sweep == 0:
                applied = apply(key_state, raw, weight_k, keys_t) * q_scale
            else:
                applied = apply(key_state, stacked(direction), weight_k, keys_t)
            applied += ridge_ref[h] * direction
            step = norm / (jnp.sum(direction * applied, axis=0, keepdims=True) + EPS)
            estimate = step * direction if estimate is None else estimate + step * direction
            if sweep + 1 < ITERS:
                residual = residual - step * applied
                fresh = jnp.sum(residual * residual, axis=0, keepdims=True)
                direction = residual + fresh / (norm + EPS) * direction
                norm = fresh
        mixed = apply(value_state, stacked(estimate), weight_v, values.T)
        mixed_ref[:, cols] = mixed.T.astype(bf16)
    mixed = mixed_ref[...]
    piece = out_ref.shape[2]
    for n in range(out_ref.shape[0]):
        out_ref[n] = dot(mixed, w_ref[:, n * piece : (n + 1) * piece]).astype(bf16)


def shards(queries, keys, values, ridges, out_weight):
    heads = ridges.shape[0]
    tokens, width = queries.shape
    spread = lax.axis_size("head")
    rows, far = lax.axis_size("y"), lax.axis_size("far")
    members = lax.axis_size("near") * lax.axis_size("core")
    piece = 2 * heads * HD // (rows * members)

    own = pl.pallas_call(
        grams,
        out_shape=jax.ShapeDtypeStruct((2 * heads, HD, HD), bf16),
        in_specs=[vmem()] * 2,
        out_specs=vmem(),
        compiler_params=params(),
        name="grams",
    )(keys, values)
    near = lax.all_to_all(own.reshape(rows * members, piece, HD), NEAR, 0, 0, tiled=True)
    near = near.reshape(rows, members, piece, HD)
    totals = pl.pallas_call(
        group_totals,
        out_shape=jax.ShapeDtypeStruct((far, rows, piece, HD), bf16),
        in_specs=[vmem()],
        out_specs=vmem(),
        compiler_params=params(),
        name="group_totals",
    )(near)
    totals = lax.all_to_all(totals, "far", 0, 0, tiled=True)
    states = pl.pallas_call(
        prefixes,
        out_shape=jax.ShapeDtypeStruct((rows, members, piece, HD), bf16),
        in_specs=[smem(), vmem(), vmem()],
        out_specs=vmem(),
        compiler_params=params(),
        name="prefixes",
    )(lax.axis_index("far").astype(jnp.int32).reshape(1), near, totals)
    states = lax.all_to_all(states.reshape(rows * members, piece, HD), NEAR, 0, 0, tiled=True)
    states = states.reshape(2 * heads, HD, HD)
    partial = pl.pallas_call(
        solve,
        out_shape=jax.ShapeDtypeStruct((spread, tokens, out_weight.shape[1] // spread), bf16),
        in_specs=[smem()] + [vmem()] * 5,
        out_specs=vmem(),
        scratch_shapes=[pltpu.VMEM((tokens, width), bf16)],
        compiler_params=params(),
        name="solve",
    )(ridges, queries, keys, values, states, out_weight)
    partial = lax.all_to_all(partial, "head", 0, 0, tiled=True)
    total = partial[0].astype(f32)
    for n in range(1, spread):
        total += partial[n].astype(f32)
    return total.astype(bf16)


def solution(mesh):
    split = Mesh(mesh.devices.reshape(4, 4, 4, 2, mesh.shape["head"]), (*SEQ, "head"))
    placed = (P(SEQ, "head"), P(SEQ, "head"), P(SEQ, "head"), P("head"), P("head", None))
    return jax.shard_map(
        shards, mesh=split, in_specs=placed, out_specs=P(SEQ, "head"), check_vma=False
    )
```

```python
import jax
import jax.numpy as jnp
from jax import lax
from jax.experimental import pallas as pl
from jax.experimental.pallas import tpu as pltpu
from jax.sharding import Mesh
from jax.sharding import PartitionSpec as P

HD = 128
SEQ = ("y", "far", "near", "core")
NEAR = ("y", "near", "core")
EPS = 1e-06
f32, bf16 = jnp.float32, jnp.bfloat16


def vmem():
    return pl.BlockSpec(memory_space=pltpu.VMEM)


def smem():
    return pl.BlockSpec(memory_space=pltpu.SMEM)


def params():
    return pltpu.CompilerParams(vmem_limit_bytes=32 * 1024 * 1024)


def halves(value):
    high = value.astype(bf16)
    return high, (value - high.astype(f32)).astype(bf16)


def pack(value):
    return (value * value * (value * jnp.abs(value))).astype(bf16)


def unpack(coded):
    coded = coded.astype(f32)
    root = jnp.sqrt(jnp.sqrt(jnp.abs(coded)))
    return jnp.where(coded < 0.0, -root, root)


def dot(left, right):
    return jnp.dot(left, right, preferred_element_type=f32)


def key_scale(keys):
    keys = keys.astype(f32)
    return lax.rsqrt(jnp.sum(keys * keys, axis=1, keepdims=True) + EPS)


def grams(k_ref, v_ref, out_ref):
    heads = k_ref.shape[1] // HD
    for h in range(heads):
        cols = slice(h * HD, (h + 1) * HD)
        keys, values = k_ref[:, cols], v_ref[:, cols]
        scale = key_scale(keys)
        kn = keys.astype(f32) * scale
        key_side = jnp.concatenate(halves(kn * scale), axis=1)
        value_side = jnp.concatenate(halves(kn), axis=1)
        key_gram = dot(keys.T, key_side)
        value_gram = dot(values.T, value_side)
        out_ref[h] = pack(key_gram[:, :HD] + key_gram[:, HD:])
        out_ref[heads + h] = pack(value_gram[:, :HD] + value_gram[:, HD:])


def group_totals(near_ref, out_ref):
    for y in range(near_ref.shape[0]):
        total = unpack(near_ref[y, 0])
        for member in range(1, near_ref.shape[1]):
            total += unpack(near_ref[y, member])
        total = pack(total)
        for far in range(out_ref.shape[0]):
            out_ref[far, y] = total


def prefixes(near_ref, far_ref, out_ref):
    mine = lax.axis_index("far")
    before = jnp.zeros(near_ref.shape[2:], f32)
    for y in range(near_ref.shape[0]):
        running = before
        for far in range(far_ref.shape[0]):
            total = unpack(far_ref[far, y])
            running += jnp.where(far < mine, total, 0.0)
            before += total
        for member in range(near_ref.shape[1]):
            out_ref[y, member] = pack(running)
            running += unpack(near_ref[y, member])


def solve(ridge_ref, q_ref, k_ref, v_ref, state_ref, w_ref, out_ref, mixed_ref):
    tokens, width = q_ref.shape
    heads = range(width // HD)
    cols = [slice(h * HD, (h + 1) * HD) for h in heads]
    causal = lax.broadcasted_iota(jnp.int32, (tokens, tokens), 0) <= lax.broadcasted_iota(
        jnp.int32, (tokens, tokens), 1
    )

    def total(left, right):
        return jnp.sum(left * right, axis=0, keepdims=True)

    def apply(keys, state, vectors, scale, payload):
        left = jnp.concatenate([keys, state[0]], axis=0)
        left = jnp.concatenate([left] * len(vectors), axis=1)
        both = dot(left, jnp.concatenate(vectors, axis=0))
        scores = jnp.where(causal, both[:tokens] * scale, 0.0).astype(bf16)
        return both[tokens:] + dot(state[1], vectors[0]) + dot(payload, scores)

    keys = [k_ref[:, c] for c in cols]
    scales = [key_scale(k) for k in keys]
    squares = [s * s for s in scales]
    raw = [q_ref[:, c].T for c in cols]
    keys_t = [k.T for k in keys]
    values_t = [v_ref[:, c].T for c in cols]
    states = [halves(unpack(state_ref[h])) for h in heads]
    floats = [r.astype(f32) for r in raw]
    q_scales = [lax.rsqrt(total(f, f) + EPS) for f in floats]
    first = [f * s for f, s in zip(floats, q_scales)]
    norms = [total(d, d) for d in first]
    applied = [
        apply(keys[h], states[h], (raw[h],), squares[h], keys_t[h]) * q_scales[h]
        + ridge_ref[h] * first[h]
        for h in heads
    ]
    steps = [norms[h] / (total(first[h], applied[h]) + EPS) for h in heads]
    residuals = [first[h] - steps[h] * applied[h] for h in heads]
    fresh = [total(r, r) for r in residuals]
    second = [residuals[h] + fresh[h] / (norms[h] + EPS) * first[h] for h in heads]
    applied = [
        apply(keys[h], states[h], halves(second[h]), squares[h], keys_t[h])
        + ridge_ref[h] * second[h]
        for h in heads
    ]
    last = [fresh[h] / (total(second[h], applied[h]) + EPS) for h in heads]
    estimates = [steps[h] * first[h] + last[h] * second[h] for h in heads]
    states = [halves(unpack(state_ref[len(heads) + h])) for h in heads]
    mixed = [
        apply(keys[h], states[h], halves(estimates[h]), scales[h], values_t[h]) for h in heads
    ]
    for h in heads:
        mixed_ref[:, cols[h]] = mixed[h].T.astype(bf16)
    mixed = mixed_ref[...]
    piece = out_ref.shape[2]
    for n in range(out_ref.shape[0]):
        out_ref[n] = dot(mixed, w_ref[:, n * piece : (n + 1) * piece]).astype(bf16)


def shards(queries, keys, values, ridges, out_weight):
    heads = ridges.shape[0]
    tokens, width = queries.shape
    spread = lax.axis_size("head")
    rows, far = lax.axis_size("y"), lax.axis_size("far")
    members = lax.axis_size("near") * lax.axis_size("core")
    piece = 2 * heads * HD // (rows * members)

    own = pl.pallas_call(
        grams,
        out_shape=jax.ShapeDtypeStruct((2 * heads, HD, HD), bf16),
        in_specs=[vmem()] * 2,
        out_specs=vmem(),
        compiler_params=params(),
        name="grams",
    )(keys, values)
    near = lax.all_to_all(own.reshape(rows * members, piece, HD), NEAR, 0, 0, tiled=True)
    near = near.reshape(rows, members, piece, HD)
    totals = pl.pallas_call(
        group_totals,
        out_shape=jax.ShapeDtypeStruct((far, rows, piece, HD), bf16),
        in_specs=[vmem()],
        out_specs=vmem(),
        compiler_params=params(),
        name="group_totals",
    )(near)
    totals = lax.all_to_all(totals, "far", 0, 0, tiled=True)
    states = pl.pallas_call(
        prefixes,
        out_shape=jax.ShapeDtypeStruct((rows, members, piece, HD), bf16),
        in_specs=[vmem(), vmem()],
        out_specs=vmem(),
        compiler_params=params(),
        name="prefixes",
    )(near, totals)
    states = lax.all_to_all(states.reshape(rows * members, piece, HD), NEAR, 0, 0, tiled=True)
    states = states.reshape(2 * heads, HD, HD)
    partial = pl.pallas_call(
        solve,
        out_shape=jax.ShapeDtypeStruct((spread, tokens, out_weight.shape[1] // spread), bf16),
        in_specs=[smem()] + [vmem()] * 5,
        out_specs=vmem(),
        scratch_shapes=[pltpu.VMEM((tokens, width), bf16)],
        compiler_params=params(),
        name="solve",
    )(ridges, queries, keys, values, states, out_weight)
    partial = lax.all_to_all(partial, "head", 0, 0, tiled=True)
    total = partial[0].astype(f32)
    for n in range(1, spread):
        total += partial[n].astype(f32)
    return total.astype(bf16)


def solution(mesh):
    split = Mesh(mesh.devices.reshape(4, 4, 4, 2, mesh.shape["head"]), (*SEQ, "head"))
    placed = (P(SEQ, "head"), P(SEQ, "head"), P(SEQ, "head"), P("head"), P("head", None))
    return jax.shard_map(
        shards, mesh=split, in_specs=placed, out_specs=P(SEQ, "head"), check_vma=False
    )
```

```python
import jax
import jax.numpy as jnp
from jax import lax
from jax.experimental import pallas as pl
from jax.experimental.pallas import tpu as pltpu
from jax.sharding import Mesh
from jax.sharding import PartitionSpec as P

HD = 128
SEQ = ("y", "far", "near", "core")
NEAR = ("y", "near", "core")
EPS = 1e-06
f32, bf16 = jnp.float32, jnp.bfloat16


def vmem():
    return pl.BlockSpec(memory_space=pltpu.VMEM)


def smem():
    return pl.BlockSpec(memory_space=pltpu.SMEM)


def params():
    return pltpu.CompilerParams(vmem_limit_bytes=32 * 1024 * 1024)


def far_groups():
    return [[near + 4 * far if far < 2 else (near + 2) % 4 + 4 * far for far in range(4)] for near in range(4)]


def turned(matrix):
    return matrix ^ (lax.axis_index("far") // 2)


def halves(value):
    high = value.astype(bf16)
    return high, (value - high.astype(f32)).astype(bf16)


def pack(value):
    return (value * value * (value * jnp.abs(value))).astype(bf16)


def unpack(coded):
    coded = coded.astype(f32)
    root = jnp.sqrt(jnp.sqrt(jnp.abs(coded)))
    return jnp.where(coded < 0.0, -root, root)


def dot(left, right):
    return jnp.dot(left, right, preferred_element_type=f32)


def key_scale(keys):
    keys = keys.astype(f32)
    return lax.rsqrt(jnp.sum(keys * keys, axis=1, keepdims=True) + EPS)


def grams(k_ref, v_ref, out_ref):
    heads = k_ref.shape[1] // HD
    for h in range(heads):
        cols = slice(h * HD, (h + 1) * HD)
        keys, values = k_ref[:, cols], v_ref[:, cols]
        scale = key_scale(keys)
        kn = keys.astype(f32) * scale
        key_side = jnp.concatenate(halves(kn * scale), axis=1)
        value_side = jnp.concatenate(halves(kn), axis=1)
        key_gram = dot(keys.T, key_side)
        value_gram = dot(values.T, value_side)
        out_ref[turned(h)] = pack(key_gram[:, :HD] + key_gram[:, HD:])
        out_ref[turned(heads + h)] = pack(value_gram[:, :HD] + value_gram[:, HD:])


def group_totals(near_ref, out_ref):
    for y in range(near_ref.shape[0]):
        total = unpack(near_ref[y, 0])
        for member in range(1, near_ref.shape[1]):
            total += unpack(near_ref[y, member])
        total = pack(total)
        for far in range(out_ref.shape[0]):
            out_ref[far, y] = total


def prefixes(near_ref, far_ref, out_ref):
    mine = lax.axis_index("far")
    before = jnp.zeros(near_ref.shape[2:], f32)
    for y in range(near_ref.shape[0]):
        running = before
        for far in range(far_ref.shape[0]):
            total = unpack(far_ref[far, y])
            running += jnp.where(far < mine, total, 0.0)
            before += total
        for member in range(near_ref.shape[1]):
            out_ref[y, member] = pack(running)
            running += unpack(near_ref[y, member])


def solve(ridge_ref, q_ref, k_ref, v_ref, state_ref, w_ref, out_ref, mixed_ref):
    tokens, width = q_ref.shape
    heads = range(width // HD)
    cols = [slice(h * HD, (h + 1) * HD) for h in heads]
    causal = lax.broadcasted_iota(jnp.int32, (tokens, tokens), 0) <= lax.broadcasted_iota(
        jnp.int32, (tokens, tokens), 1
    )

    def total(left, right):
        return jnp.sum(left * right, axis=0, keepdims=True)

    def apply(keys, state, vectors, scale, payload):
        left = jnp.concatenate([keys, state[0]], axis=0)
        left = jnp.concatenate([left] * len(vectors), axis=1)
        both = dot(left, jnp.concatenate(vectors, axis=0))
        scores = jnp.where(causal, both[:tokens] * scale, 0.0).astype(bf16)
        return both[tokens:] + dot(state[1], vectors[0]) + dot(payload, scores)

    keys = [k_ref[:, c] for c in cols]
    scales = [key_scale(k) for k in keys]
    squares = [s * s for s in scales]
    raw = [q_ref[:, c].T for c in cols]
    keys_t = [k.T for k in keys]
    values_t = [v_ref[:, c].T for c in cols]
    states = [halves(unpack(state_ref[turned(h)])) for h in heads]
    floats = [r.astype(f32) for r in raw]
    q_scales = [lax.rsqrt(total(f, f) + EPS) for f in floats]
    first = [f * s for f, s in zip(floats, q_scales)]
    norms = [total(d, d) for d in first]
    applied = [
        apply(keys[h], states[h], (raw[h],), squares[h], keys_t[h]) * q_scales[h]
        + ridge_ref[h] * first[h]
        for h in heads
    ]
    steps = [norms[h] / (total(first[h], applied[h]) + EPS) for h in heads]
    residuals = [first[h] - steps[h] * applied[h] for h in heads]
    fresh = [total(r, r) for r in residuals]
    second = [residuals[h] + fresh[h] / (norms[h] + EPS) * first[h] for h in heads]
    applied = [
        apply(keys[h], states[h], halves(second[h]), squares[h], keys_t[h])
        + ridge_ref[h] * second[h]
        for h in heads
    ]
    last = [fresh[h] / (total(second[h], applied[h]) + EPS) for h in heads]
    estimates = [steps[h] * first[h] + last[h] * second[h] for h in heads]
    states = [halves(unpack(state_ref[turned(len(heads) + h)])) for h in heads]
    mixed = [
        apply(keys[h], states[h], halves(estimates[h]), scales[h], values_t[h]) for h in heads
    ]
    for h in heads:
        mixed_ref[:, cols[h]] = mixed[h].T.astype(bf16)
    mixed = mixed_ref[...]
    piece = out_ref.shape[2]
    for n in range(out_ref.shape[0]):
        out_ref[n] = dot(mixed, w_ref[:, n * piece : (n + 1) * piece]).astype(bf16)


def shards(queries, keys, values, ridges, out_weight):
    heads = ridges.shape[0]
    tokens, width = queries.shape
    spread = lax.axis_size("head")
    rows, far = lax.axis_size("y"), lax.axis_size("far")
    members = lax.axis_size("near") * lax.axis_size("core")
    piece = 2 * heads * HD // (rows * members)

    own = pl.pallas_call(
        grams,
        out_shape=jax.ShapeDtypeStruct((2 * heads, HD, HD), bf16),
        in_specs=[vmem()] * 2,
        out_specs=vmem(),
        compiler_params=params(),
        name="grams",
    )(keys, values)
    near = lax.all_to_all(own.reshape(rows * members, piece, HD), NEAR, 0, 0, tiled=True)
    near = near.reshape(rows, members, piece, HD)
    totals = pl.pallas_call(
        group_totals,
        out_shape=jax.ShapeDtypeStruct((far, rows, piece, HD), bf16),
        in_specs=[vmem()],
        out_specs=vmem(),
        compiler_params=params(),
        name="group_totals",
    )(near)
    totals = lax.all_to_all(
        totals, ("far", "near"), 0, 0, axis_index_groups=far_groups(), tiled=True
    )
    states = pl.pallas_call(
        prefixes,
        out_shape=jax.ShapeDtypeStruct((rows, members, piece, HD), bf16),
        in_specs=[vmem(), vmem()],
        out_specs=vmem(),
        compiler_params=params(),
        name="prefixes",
    )(near, totals)
    states = lax.all_to_all(states.reshape(rows * members, piece, HD), NEAR, 0, 0, tiled=True)
    states = states.reshape(2 * heads, HD, HD)
    partial = pl.pallas_call(
        solve,
        out_shape=jax.ShapeDtypeStruct((spread, tokens, out_weight.shape[1] // spread), bf16),
        in_specs=[smem()] + [vmem()] * 5,
        out_specs=vmem(),
        scratch_shapes=[pltpu.VMEM((tokens, width), bf16)],
        compiler_params=params(),
        name="solve",
    )(ridges, queries, keys, values, states, out_weight)
    partial = lax.all_to_all(partial, "head", 0, 0, tiled=True)
    total = partial[0].astype(f32)
    for n in range(1, spread):
        total += partial[n].astype(f32)
    return total.astype(bf16)


def solution(mesh):
    split = Mesh(mesh.devices.reshape(4, 4, 4, 2, mesh.shape["head"]), (*SEQ, "head"))
    placed = (P(SEQ, "head"), P(SEQ, "head"), P(SEQ, "head"), P("head"), P("head", None))
    return jax.shard_map(
        shards, mesh=split, in_specs=placed, out_specs=P(SEQ, "head"), check_vma=False
    )
```

```python
import jax
import jax.numpy as jnp
from jax import lax
from jax.experimental import pallas as pl
from jax.experimental.pallas import tpu as pltpu
from jax.sharding import Mesh
from jax.sharding import PartitionSpec as P

HD = 128
SEQ = ("y", "far", "near", "core")
NEAR = ("y", "near", "core")
EPS = 1e-06
ROWS = 4
f32, bf16 = jnp.float32, jnp.bfloat16


def vmem():
    return pl.BlockSpec(memory_space=pltpu.VMEM)


def smem():
    return pl.BlockSpec(memory_space=pltpu.SMEM)


def params():
    return pltpu.CompilerParams(vmem_limit_bytes=32 * 1024 * 1024)


def far_groups():
    return [[near + 4 * far if far < 2 else (near + 2) % 4 + 4 * far for far in range(4)] for near in range(4)]


def turned(rows, turns):
    size = rows.shape[0] // (2 * turns)
    parts = [rows[n * size : (n + 1) * size] for n in range(2 * turns)]
    upper = lax.axis_index("far") >= 2
    return jnp.concatenate(
        [jnp.where(upper, parts[n ^ 1], parts[n]) for n in range(2 * turns)], axis=0
    )


def position(axis):
    return lax.broadcasted_iota(jnp.int32, (HD, HD), axis)


def halves(value):
    high = value.astype(bf16)
    return high, (value - high.astype(f32)).astype(bf16)


def pack(value):
    return (value * value * (value * jnp.abs(value))).astype(bf16)


def unpack(coded):
    coded = coded.astype(f32)
    root = jnp.sqrt(jnp.sqrt(jnp.abs(coded)))
    return jnp.where(coded < 0.0, -root, root)


def dot(left, right):
    return jnp.dot(left, right, preferred_element_type=f32)


def key_scale(keys):
    keys = keys.astype(f32)
    return lax.rsqrt(jnp.sum(keys * keys, axis=1, keepdims=True) + EPS)


def grams(k_ref, v_ref, out_ref, rows_ref):
    heads = k_ref.shape[1] // HD
    squares = []
    for h in range(heads):
        cols = slice(h * HD, (h + 1) * HD)
        keys, values = k_ref[:, cols], v_ref[:, cols]
        scale = key_scale(keys)
        kn = keys.astype(f32) * scale
        key_side = jnp.concatenate(halves(kn * scale), axis=1)
        value_side = jnp.concatenate(halves(kn), axis=1)
        key_gram = dot(keys.T, key_side)
        value_gram = dot(values.T, value_side)
        squares.append(key_gram[:, :HD] + key_gram[:, HD:])
        rows_ref[h * HD : (h + 1) * HD] = value_gram[:, :HD] + value_gram[:, HD:]
    tail = (heads + heads // 2) * HD
    rows_ref[tail:] = jnp.zeros((rows_ref.shape[0] - tail, HD), f32)
    for n in range(heads // 2):
        one, other = squares[2 * n], squares[2 * n + 1]
        at = (heads + n) * HD
        rows_ref[at : at + HD] = jnp.where(position(0) <= position(1), one, other)
        rows_ref[tail + n : tail + n + 1] = jnp.sum(
            jnp.where(position(0) == position(1), other, 0.0), axis=0, keepdims=True
        )
    out_ref[...] = pack(turned(rows_ref[...], ROWS))


def group_totals(near_ref, out_ref, terms_ref, total_ref):
    terms_ref[...] = unpack(near_ref[...])
    piece = total_ref.shape[0] // ROWS
    members = near_ref.shape[0] // total_ref.shape[0]
    for y in range(ROWS):
        at = y * members * piece
        total = terms_ref[at : at + piece]
        for member in range(1, members):
            total += terms_ref[at + member * piece : at + (member + 1) * piece]
        total_ref[y * piece : (y + 1) * piece] = total
    total = pack(total_ref[...])
    for far in range(out_ref.shape[0]):
        out_ref[far] = total


def prefixes(terms_ref, far_ref, out_ref, total_ref, rows_ref):
    mine = lax.axis_index("far")
    quarters, rows = far_ref.shape[:2]
    piece = rows // ROWS
    members = terms_ref.shape[0] // rows
    for far in range(quarters):
        total_ref[far * rows : (far + 1) * rows] = unpack(far_ref[far])
    before = jnp.zeros((piece, HD), f32)
    for y in range(ROWS):
        running = before
        for far in range(quarters):
            at = far * rows + y * piece
            total = total_ref[at : at + piece]
            running += jnp.where(far < mine, total, 0.0)
            before += total
        for member in range(members):
            at = (y * members + member) * piece
            rows_ref[at : at + piece] = running
            running += terms_ref[at : at + piece]
    out_ref[...] = pack(rows_ref[...])


def solve(ridge_ref, q_ref, k_ref, v_ref, state_ref, w_ref, out_ref, mixed_ref, rows_ref):
    tokens, width = q_ref.shape
    heads = range(width // HD)
    cols = [slice(h * HD, (h + 1) * HD) for h in heads]
    causal = lax.broadcasted_iota(jnp.int32, (tokens, tokens), 0) <= lax.broadcasted_iota(
        jnp.int32, (tokens, tokens), 1
    )

    def total(left, right):
        return jnp.sum(left * right, axis=0, keepdims=True)

    def apply(keys, state, vectors, scale, payload):
        left = jnp.concatenate([keys, state[0]], axis=0)
        left = jnp.concatenate([left] * len(vectors), axis=1)
        both = dot(left, jnp.concatenate(vectors, axis=0))
        scores = jnp.where(causal, both[:tokens] * scale, 0.0).astype(bf16)
        return both[tokens:] + dot(state[1], vectors[0]) + dot(payload, scores)

    keys = [k_ref[:, c] for c in cols]
    scales = [key_scale(k) for k in keys]
    squares = [s * s for s in scales]
    raw = [q_ref[:, c].T for c in cols]
    keys_t = [k.T for k in keys]
    values_t = [v_ref[:, c].T for c in cols]
    rows_ref[...] = turned(unpack(state_ref[...]), ROWS)
    upper, diagonal = position(0) <= position(1), position(0) == position(1)
    tail = (len(heads) + len(heads) // 2) * HD
    states = []
    for n in range(len(heads) // 2):
        at = (len(heads) + n) * HD
        both = rows_ref[at : at + HD]
        mirrored = both.T
        states.append(halves(jnp.where(upper, both, mirrored)))
        other = jnp.where(upper, mirrored, both)
        states.append(halves(jnp.where(diagonal, rows_ref[tail + n : tail + n + 1], other)))
    floats = [r.astype(f32) for r in raw]
    q_scales = [lax.rsqrt(total(f, f) + EPS) for f in floats]
    first = [f * s for f, s in zip(floats, q_scales)]
    norms = [total(d, d) for d in first]
    applied = [
        apply(keys[h], states[h], (raw[h],), squares[h], keys_t[h]) * q_scales[h]
        + ridge_ref[h] * first[h]
        for h in heads
    ]
    steps = [norms[h] / (total(first[h], applied[h]) + EPS) for h in heads]
    residuals = [first[h] - steps[h] * applied[h] for h in heads]
    fresh = [total(r, r) for r in residuals]
    second = [residuals[h] + fresh[h] / (norms[h] + EPS) * first[h] for h in heads]
    applied = [
        apply(keys[h], states[h], halves(second[h]), squares[h], keys_t[h])
        + ridge_ref[h] * second[h]
        for h in heads
    ]
    last = [fresh[h] / (total(second[h], applied[h]) + EPS) for h in heads]
    estimates = [steps[h] * first[h] + last[h] * second[h] for h in heads]
    states = [halves(rows_ref[h * HD : (h + 1) * HD]) for h in heads]
    mixed = [
        apply(keys[h], states[h], halves(estimates[h]), scales[h], values_t[h]) for h in heads
    ]
    for h in heads:
        mixed_ref[:, cols[h]] = mixed[h].T.astype(bf16)
    mixed = mixed_ref[...]
    piece = out_ref.shape[2]
    for n in range(out_ref.shape[0]):
        out_ref[n] = dot(mixed, w_ref[:, n * piece : (n + 1) * piece]).astype(bf16)


def shards(queries, keys, values, ridges, out_weight):
    heads = ridges.shape[0]
    tokens, width = queries.shape
    spread, quarters = lax.axis_size("head"), lax.axis_size("far")
    holders = ROWS * lax.axis_size("near") * lax.axis_size("core")
    piece = 2 * pl.cdiv((heads + heads // 2) * HD + heads // 2, 2 * holders)

    def exchange(rows):
        rows = rows.reshape(holders, piece // 2, 2, HD)
        return lax.all_to_all(rows, NEAR, 0, 0, tiled=True).reshape(holders * piece, HD)

    def scratch(count):
        return pltpu.VMEM((count * piece, HD), f32)

    rows = jax.ShapeDtypeStruct((holders * piece, HD), bf16)
    own = pl.pallas_call(
        grams,
        out_shape=rows,
        in_specs=[vmem()] * 2,
        out_specs=vmem(),
        scratch_shapes=[scratch(holders)],
        compiler_params=params(),
        name="grams",
    )(keys, values)
    totals, terms = pl.pallas_call(
        group_totals,
        out_shape=(
            jax.ShapeDtypeStruct((quarters, ROWS * piece, HD), bf16),
            jax.ShapeDtypeStruct(rows.shape, f32),
        ),
        in_specs=[vmem()],
        out_specs=(vmem(), vmem()),
        scratch_shapes=[scratch(ROWS)],
        compiler_params=params(),
        name="group_totals",
    )(exchange(own))
    totals = lax.all_to_all(
        totals, ("far", "near"), 0, 0, axis_index_groups=far_groups(), tiled=True
    )
    states = pl.pallas_call(
        prefixes,
        out_shape=rows,
        in_specs=[vmem(), vmem()],
        out_specs=vmem(),
        scratch_shapes=[scratch(quarters * ROWS), scratch(holders)],
        compiler_params=params(),
        name="prefixes",
    )(terms, totals)
    partial = pl.pallas_call(
        solve,
        out_shape=jax.ShapeDtypeStruct((spread, tokens, out_weight.shape[1] // spread), bf16),
        in_specs=[smem()] + [vmem()] * 5,
        out_specs=vmem(),
        scratch_shapes=[pltpu.VMEM((tokens, width), bf16), scratch(holders)],
        compiler_params=params(),
        name="solve",
    )(ridges, queries, keys, values, exchange(states), out_weight)
    partial = lax.all_to_all(partial, "head", 0, 0, tiled=True)
    total = partial[0].astype(f32)
    for n in range(1, spread):
        total += partial[n].astype(f32)
    return total.astype(bf16)


def solution(mesh):
    split = Mesh(mesh.devices.reshape(ROWS, 4, 4, 2, mesh.shape["head"]), (*SEQ, "head"))
    placed = (P(SEQ, "head"), P(SEQ, "head"), P(SEQ, "head"), P("head"), P("head", None))
    return jax.shard_map(
        shards, mesh=split, in_specs=placed, out_specs=P(SEQ, "head"), check_vma=False
    )
```

```python
import jax
import jax.numpy as jnp
from jax import lax
from jax.experimental import pallas as pl
from jax.experimental.pallas import tpu as pltpu
from jax.sharding import Mesh
from jax.sharding import PartitionSpec as P

HD = 128
SEQ = ("y", "far", "near", "core")
EPS = 1e-06
ROWS = 4
Y_ORDER, NEAR_ORDER, CORE_ORDER = (2, 3, 0, 1), (2, 3, 0, 1), (1, 0)
FAR_ORDER, HEAD_ORDER = (2, 0, 3, 1), (2, 3, 1, 0)
MEMBERS = [NEAR_ORDER.index(near) * 2 + CORE_ORDER.index(core) for near in range(4) for core in range(2)]
f32, bf16 = jnp.float32, jnp.bfloat16


def vmem():
    return pl.BlockSpec(memory_space=pltpu.VMEM)


def smem():
    return pl.BlockSpec(memory_space=pltpu.SMEM)


def params():
    return pltpu.CompilerParams(vmem_limit_bytes=32 * 1024 * 1024)


def far_groups():
    return [[near + 4 * far if far < 2 else (near + 2) % 4 + 4 * far for far in FAR_ORDER] for near in range(4)]


def near_groups():
    return [
        [((y * 4 + far) * 4 + near) * 2 + core for y in Y_ORDER for near in NEAR_ORDER for core in CORE_ORDER]
        for far in range(4)
    ]


def turned(rows, turns):
    size = rows.shape[0] // (2 * turns)
    parts = [rows[n * size : (n + 1) * size] for n in range(2 * turns)]
    upper = lax.axis_index("far") >= 2
    return jnp.concatenate(
        [jnp.where(upper, parts[n ^ 1], parts[n]) for n in range(2 * turns)], axis=0
    )


def position(axis):
    return lax.broadcasted_iota(jnp.int32, (HD, HD), axis)


def halves(value):
    high = value.astype(bf16)
    return high, (value - high.astype(f32)).astype(bf16)


def pack(value):
    return (value * value * (value * jnp.abs(value))).astype(bf16)


def unpack(coded):
    coded = coded.astype(f32)
    root = jnp.sqrt(jnp.sqrt(jnp.abs(coded)))
    return jnp.where(coded < 0.0, -root, root)


def dot(left, right):
    return jnp.dot(left, right, preferred_element_type=f32)


def key_scale(keys):
    keys = keys.astype(f32)
    return lax.rsqrt(jnp.sum(keys * keys, axis=1, keepdims=True) + EPS)


def grams(k_ref, v_ref, out_ref, keys_ref, values_ref, rows_ref):
    heads = k_ref.shape[1] // HD
    keys_ref[...] = k_ref[...]
    values_ref[...] = v_ref[...]
    squares = []
    for h in range(heads):
        cols = slice(h * HD, (h + 1) * HD)
        keys, values = k_ref[:, cols], v_ref[:, cols]
        scale = key_scale(keys)
        kn = keys.astype(f32) * scale
        key_side = jnp.concatenate(halves(kn * scale), axis=1)
        value_side = jnp.concatenate(halves(kn), axis=1)
        key_gram = dot(keys.T, key_side)
        value_gram = dot(values.T, value_side)
        squares.append(key_gram[:, :HD] + key_gram[:, HD:])
        rows_ref[h * HD : (h + 1) * HD] = value_gram[:, :HD] + value_gram[:, HD:]
    tail = (heads + heads // 2) * HD
    rows_ref[tail:] = jnp.zeros((rows_ref.shape[0] - tail, HD), f32)
    for n in range(heads // 2):
        one, other = squares[2 * n], squares[2 * n + 1]
        at = (heads + n) * HD
        rows_ref[at : at + HD] = jnp.where(position(0) <= position(1), one, other)
        rows_ref[tail + n : tail + n + 1] = jnp.sum(
            jnp.where(position(0) == position(1), other, 0.0), axis=0, keepdims=True
        )
    out_ref[...] = pack(turned(rows_ref[...], ROWS))


def group_totals(near_ref, out_ref, terms_ref, total_ref):
    terms_ref[...] = unpack(near_ref[...])
    piece = total_ref.shape[0] // ROWS
    members = near_ref.shape[0] // total_ref.shape[0]
    for y in range(ROWS):
        at = Y_ORDER.index(y) * members * piece
        total = terms_ref[at : at + piece]
        for member in range(1, members):
            total += terms_ref[at + member * piece : at + (member + 1) * piece]
        total_ref[y * piece : (y + 1) * piece] = total
    total = pack(total_ref[...])
    for far in range(out_ref.shape[0]):
        out_ref[far] = total


def prefixes(terms_ref, far_ref, out_ref, total_ref, rows_ref):
    mine = lax.axis_index("far")
    quarters, rows = far_ref.shape[:2]
    piece = rows // ROWS
    for far in range(quarters):
        total_ref[far * rows : (far + 1) * rows] = unpack(far_ref[far])
    before = jnp.zeros((piece, HD), f32)
    for y in range(ROWS):
        running = before
        for far in range(quarters):
            at = far * rows + y * piece
            total = total_ref[at : at + piece]
            running += jnp.where(FAR_ORDER[far] < mine, total, 0.0)
            before += total
        for member in MEMBERS:
            at = (Y_ORDER.index(y) * len(MEMBERS) + member) * piece
            rows_ref[at : at + piece] = running
            running += terms_ref[at : at + piece]
    out_ref[...] = pack(rows_ref[...])


def solve(ridge_ref, q_ref, k_ref, v_ref, state_ref, w_ref, out_ref, mixed_ref, rows_ref):
    tokens, width = q_ref.shape
    heads = range(width // HD)
    cols = [slice(h * HD, (h + 1) * HD) for h in heads]
    causal = lax.broadcasted_iota(jnp.int32, (tokens, tokens), 0) <= lax.broadcasted_iota(
        jnp.int32, (tokens, tokens), 1
    )

    def total(left, right):
        return jnp.sum(left * right, axis=0, keepdims=True)

    def apply(keys, state, vectors, scale, payload):
        left = jnp.concatenate([keys, state[0]], axis=0)
        left = jnp.concatenate([left] * len(vectors), axis=1)
        both = dot(left, jnp.concatenate(vectors, axis=0))
        scores = jnp.where(causal, both[:tokens] * scale, 0.0).astype(bf16)
        return both[tokens:] + dot(state[1], vectors[0]) + dot(payload, scores)

    keys = [k_ref[:, c] for c in cols]
    scales = [key_scale(k) for k in keys]
    squares = [s * s for s in scales]
    raw = [q_ref[:, c].T for c in cols]
    keys_t = [k.T for k in keys]
    values_t = [v_ref[:, c].T for c in cols]
    rows_ref[...] = turned(unpack(state_ref[...]), ROWS)
    upper, diagonal = position(0) <= position(1), position(0) == position(1)
    tail = (len(heads) + len(heads) // 2) * HD
    states = []
    for n in range(len(heads) // 2):
        at = (len(heads) + n) * HD
        both = rows_ref[at : at + HD]
        mirrored = both.T
        states.append(halves(jnp.where(upper, both, mirrored)))
        other = jnp.where(upper, mirrored, both)
        states.append(halves(jnp.where(diagonal, rows_ref[tail + n : tail + n + 1], other)))
    floats = [r.astype(f32) for r in raw]
    q_scales = [lax.rsqrt(total(f, f) + EPS) for f in floats]
    first = [f * s for f, s in zip(floats, q_scales)]
    norms = [total(d, d) for d in first]
    applied = [
        apply(keys[h], states[h], (raw[h],), squares[h], keys_t[h]) * q_scales[h]
        + ridge_ref[h] * first[h]
        for h in heads
    ]
    steps = [norms[h] / (total(first[h], applied[h]) + EPS) for h in heads]
    residuals = [first[h] - steps[h] * applied[h] for h in heads]
    fresh = [total(r, r) for r in residuals]
    second = [residuals[h] + fresh[h] / (norms[h] + EPS) * first[h] for h in heads]
    applied = [
        apply(keys[h], states[h], halves(second[h]), squares[h], keys_t[h])
        + ridge_ref[h] * second[h]
        for h in heads
    ]
    last = [fresh[h] / (total(second[h], applied[h]) + EPS) for h in heads]
    estimates = [steps[h] * first[h] + last[h] * second[h] for h in heads]
    states = [halves(rows_ref[h * HD : (h + 1) * HD]) for h in heads]
    mixed = [
        apply(keys[h], states[h], halves(estimates[h]), scales[h], values_t[h]) for h in heads
    ]
    for h in heads:
        mixed_ref[:, cols[h]] = mixed[h].T.astype(bf16)
    mixed = mixed_ref[...]
    piece = out_ref.shape[2]
    for n in range(out_ref.shape[0]):
        at = HEAD_ORDER[n] * piece
        out_ref[n] = dot(mixed, w_ref[:, at : at + piece]).astype(bf16)


def shards(queries, keys, values, ridges, out_weight):
    heads = ridges.shape[0]
    tokens, width = queries.shape
    spread, quarters = lax.axis_size("head"), lax.axis_size("far")
    holders = ROWS * lax.axis_size("near") * lax.axis_size("core")
    piece = 2 * pl.cdiv((heads + heads // 2) * HD + heads // 2, 2 * holders)

    def exchange(rows):
        rows = rows.reshape(holders, piece // 2, 2, HD)
        rows = lax.all_to_all(rows, SEQ, 0, 0, axis_index_groups=near_groups(), tiled=True)
        return rows.reshape(holders * piece, HD)

    def scratch(count):
        return pltpu.VMEM((count * piece, HD), f32)

    rows = jax.ShapeDtypeStruct((holders * piece, HD), bf16)
    held = jax.ShapeDtypeStruct((tokens, width), bf16)
    own, keys, values = pl.pallas_call(
        grams,
        out_shape=(rows, held, held),
        in_specs=[vmem()] * 2,
        out_specs=(vmem(),) * 3,
        scratch_shapes=[scratch(holders)],
        compiler_params=params(),
        name="grams",
    )(keys, values)
    totals, terms = pl.pallas_call(
        group_totals,
        out_shape=(
            jax.ShapeDtypeStruct((quarters, ROWS * piece, HD), bf16),
            jax.ShapeDtypeStruct(rows.shape, f32),
        ),
        in_specs=[vmem()],
        out_specs=(vmem(), vmem()),
        scratch_shapes=[scratch(ROWS)],
        compiler_params=params(),
        name="group_totals",
    )(exchange(own))
    totals = lax.all_to_all(
        totals, ("far", "near"), 0, 0, axis_index_groups=far_groups(), tiled=True
    )
    states = pl.pallas_call(
        prefixes,
        out_shape=rows,
        in_specs=[vmem(), vmem()],
        out_specs=vmem(),
        scratch_shapes=[scratch(quarters * ROWS), scratch(holders)],
        compiler_params=params(),
        name="prefixes",
    )(terms, totals)
    partial = pl.pallas_call(
        solve,
        out_shape=jax.ShapeDtypeStruct((spread, tokens, out_weight.shape[1] // spread), bf16),
        in_specs=[smem()] + [vmem()] * 5,
        out_specs=vmem(),
        scratch_shapes=[pltpu.VMEM((tokens, width), bf16), scratch(holders)],
        compiler_params=params(),
        name="solve",
    )(ridges, queries, keys, values, exchange(states), out_weight)
    partial = lax.all_to_all(
        partial, "head", 0, 0, axis_index_groups=[HEAD_ORDER], tiled=True
    )
    total = partial[0].astype(f32)
    for n in range(1, spread):
        total += partial[n].astype(f32)
    return total.astype(bf16)


def solution(mesh):
    split = Mesh(mesh.devices.reshape(ROWS, 4, 4, 2, mesh.shape["head"]), (*SEQ, "head"))
    placed = (P(SEQ, "head"), P(SEQ, "head"), P(SEQ, "head"), P("head"), P("head", None))
    return jax.shard_map(
        shards, mesh=split, in_specs=placed, out_specs=P(SEQ, "head"), check_vma=False
    )
```

```python
import jax
import jax.numpy as jnp
from jax import lax
from jax.experimental import pallas as pl
from jax.experimental.pallas import tpu as pltpu
from jax.sharding import Mesh
from jax.sharding import PartitionSpec as P

HD = 128
SEQ = ("y", "far", "near", "core")
EPS = 1e-06
ROWS = 4
Y_ORDER, NEAR_ORDER, CORE_ORDER = (2, 1, 0, 3), (2, 3, 0, 1), (1, 0)
FAR_ORDER, HEAD_ORDER = (2, 0, 3, 1), (2, 3, 1, 0)
MEMBERS = [NEAR_ORDER.index(near) * 2 + CORE_ORDER.index(core) for near in range(4) for core in range(2)]
f32, bf16 = jnp.float32, jnp.bfloat16


def vmem():
    return pl.BlockSpec(memory_space=pltpu.VMEM)


def smem():
    return pl.BlockSpec(memory_space=pltpu.SMEM)


def params():
    return pltpu.CompilerParams(vmem_limit_bytes=32 * 1024 * 1024)


def far_groups():
    return [[near + 4 * far if far < 2 else (near + 2) % 4 + 4 * far for far in FAR_ORDER] for near in range(4)]


def near_groups():
    return [
        [((y * 4 + far) * 4 + near) * 2 + core for y in Y_ORDER for near in NEAR_ORDER for core in CORE_ORDER]
        for far in range(4)
    ]


def turned(rows, turns):
    size = rows.shape[0] // (2 * turns)
    parts = [rows[n * size : (n + 1) * size] for n in range(2 * turns)]
    upper = lax.axis_index("far") >= 2
    return jnp.concatenate(
        [jnp.where(upper, parts[n ^ 1], parts[n]) for n in range(2 * turns)], axis=0
    )


def position(axis):
    return lax.broadcasted_iota(jnp.int32, (HD, HD), axis)


def halves(value):
    high = value.astype(bf16)
    return high, (value - high.astype(f32)).astype(bf16)


def pack(value):
    return (value * value * (value * jnp.abs(value))).astype(bf16)


def unpack(coded):
    coded = coded.astype(f32)
    root = jnp.sqrt(jnp.sqrt(jnp.abs(coded)))
    return jnp.where(coded < 0.0, -root, root)


def dot(left, right):
    return jnp.dot(left, right, preferred_element_type=f32)


def key_scale(keys):
    keys = keys.astype(f32)
    return lax.rsqrt(jnp.sum(keys * keys, axis=1, keepdims=True) + EPS)


def grams(k_ref, v_ref, out_ref, keys_ref, values_ref, rows_ref):
    heads = k_ref.shape[1] // HD
    keys_ref[...] = k_ref[...]
    values_ref[...] = v_ref[...]
    squares = []
    for h in range(heads):
        cols = slice(h * HD, (h + 1) * HD)
        keys, values = k_ref[:, cols], v_ref[:, cols]
        scale = key_scale(keys)
        kn = keys.astype(f32) * scale
        key_side = jnp.concatenate(halves(kn * scale), axis=1)
        value_side = jnp.concatenate(halves(kn), axis=1)
        key_gram = dot(keys.T, key_side)
        value_gram = dot(values.T, value_side)
        squares.append(key_gram[:, :HD] + key_gram[:, HD:])
        rows_ref[h * HD : (h + 1) * HD] = value_gram[:, :HD] + value_gram[:, HD:]
    tail = (heads + heads // 2) * HD
    rows_ref[tail:] = jnp.zeros((rows_ref.shape[0] - tail, HD), f32)
    for n in range(heads // 2):
        one, other = squares[2 * n], squares[2 * n + 1]
        at = (heads + n) * HD
        rows_ref[at : at + HD] = jnp.where(position(0) <= position(1), one, other)
        rows_ref[tail + n : tail + n + 1] = jnp.sum(
            jnp.where(position(0) == position(1), other, 0.0), axis=0, keepdims=True
        )
    out_ref[...] = pack(turned(rows_ref[...], ROWS))


def group_totals(near_ref, out_ref, terms_ref, total_ref):
    terms_ref[...] = unpack(near_ref[...])
    piece = total_ref.shape[0] // ROWS
    members = near_ref.shape[0] // total_ref.shape[0]
    for y in range(ROWS):
        at = Y_ORDER.index(y) * members * piece
        total = terms_ref[at : at + piece]
        for member in range(1, members):
            total += terms_ref[at + member * piece : at + (member + 1) * piece]
        total_ref[y * piece : (y + 1) * piece] = total
    total = pack(total_ref[...])
    for far in range(out_ref.shape[0]):
        out_ref[far] = total


def prefixes(terms_ref, far_ref, out_ref, total_ref, rows_ref):
    mine = lax.axis_index("far")
    quarters, rows = far_ref.shape[:2]
    piece = rows // ROWS
    for far in range(quarters):
        total_ref[far * rows : (far + 1) * rows] = unpack(far_ref[far])
    before = jnp.zeros((piece, HD), f32)
    for y in range(ROWS):
        running = before
        for far in range(quarters):
            at = far * rows + y * piece
            total = total_ref[at : at + piece]
            running += jnp.where(FAR_ORDER[far] < mine, total, 0.0)
            before += total
        for member in MEMBERS:
            at = (Y_ORDER.index(y) * len(MEMBERS) + member) * piece
            rows_ref[at : at + piece] = running
            running += terms_ref[at : at + piece]
    out_ref[...] = pack(rows_ref[...])


def solve(ridge_ref, q_ref, k_ref, v_ref, state_ref, w_ref, out_ref, mixed_ref, rows_ref):
    tokens, width = q_ref.shape
    heads = range(width // HD)
    cols = [slice(h * HD, (h + 1) * HD) for h in heads]
    causal = lax.broadcasted_iota(jnp.int32, (tokens, tokens), 0) <= lax.broadcasted_iota(
        jnp.int32, (tokens, tokens), 1
    )

    def total(left, right):
        return jnp.sum(left * right, axis=0, keepdims=True)

    def apply(keys, state, vectors, scale, payload):
        left = jnp.concatenate([keys, state[0]], axis=0)
        left = jnp.concatenate([left] * len(vectors), axis=1)
        both = dot(left, jnp.concatenate(vectors, axis=0))
        scores = jnp.where(causal, both[:tokens] * scale, 0.0).astype(bf16)
        return both[tokens:] + dot(state[1], vectors[0]) + dot(payload, scores)

    keys = [k_ref[:, c] for c in cols]
    scales = [key_scale(k) for k in keys]
    squares = [s * s for s in scales]
    raw = [q_ref[:, c].T for c in cols]
    keys_t = [k.T for k in keys]
    values_t = [v_ref[:, c].T for c in cols]
    rows_ref[...] = turned(unpack(state_ref[...]), ROWS)
    upper, diagonal = position(0) <= position(1), position(0) == position(1)
    tail = (len(heads) + len(heads) // 2) * HD
    states = []
    for n in range(len(heads) // 2):
        at = (len(heads) + n) * HD
        both = rows_ref[at : at + HD]
        mirrored = both.T
        states.append(halves(jnp.where(upper, both, mirrored)))
        other = jnp.where(upper, mirrored, both)
        states.append(halves(jnp.where(diagonal, rows_ref[tail + n : tail + n + 1], other)))
    floats = [r.astype(f32) for r in raw]
    q_scales = [lax.rsqrt(total(f, f) + EPS) for f in floats]
    first = [f * s for f, s in zip(floats, q_scales)]
    norms = [total(d, d) for d in first]
    applied = [
        apply(keys[h], states[h], (raw[h],), squares[h], keys_t[h]) * q_scales[h]
        + ridge_ref[h] * first[h]
        for h in heads
    ]
    steps = [norms[h] / (total(first[h], applied[h]) + EPS) for h in heads]
    residuals = [first[h] - steps[h] * applied[h] for h in heads]
    fresh = [total(r, r) for r in residuals]
    second = [residuals[h] + fresh[h] / (norms[h] + EPS) * first[h] for h in heads]
    applied = [
        apply(keys[h], states[h], halves(second[h]), squares[h], keys_t[h])
        + ridge_ref[h] * second[h]
        for h in heads
    ]
    last = [fresh[h] / (total(second[h], applied[h]) + EPS) for h in heads]
    estimates = [steps[h] * first[h] + last[h] * second[h] for h in heads]
    states = [halves(rows_ref[h * HD : (h + 1) * HD]) for h in heads]
    mixed = [
        apply(keys[h], states[h], halves(estimates[h]), scales[h], values_t[h]) for h in heads
    ]
    for h in heads:
        mixed_ref[:, cols[h]] = mixed[h].T.astype(bf16)
    mixed = mixed_ref[...]
    piece = out_ref.shape[2]
    for n in range(out_ref.shape[0]):
        at = HEAD_ORDER[n] * piece
        out_ref[n] = dot(mixed, w_ref[:, at : at + piece]).astype(bf16)


def shards(queries, keys, values, ridges, out_weight):
    heads = ridges.shape[0]
    tokens, width = queries.shape
    spread, quarters = lax.axis_size("head"), lax.axis_size("far")
    holders = ROWS * lax.axis_size("near") * lax.axis_size("core")
    piece = 2 * pl.cdiv((heads + heads // 2) * HD + heads // 2, 2 * holders)

    def exchange(rows):
        rows = rows.reshape(holders, piece // 2, 2, HD)
        rows = lax.all_to_all(rows, SEQ, 0, 0, axis_index_groups=near_groups(), tiled=True)
        return rows.reshape(holders * piece, HD)

    def scratch(count):
        return pltpu.VMEM((count * piece, HD), f32)

    rows = jax.ShapeDtypeStruct((holders * piece, HD), bf16)
    held = jax.ShapeDtypeStruct((tokens, width), bf16)
    own, keys, values = pl.pallas_call(
        grams,
        out_shape=(rows, held, held),
        in_specs=[vmem()] * 2,
        out_specs=(vmem(),) * 3,
        scratch_shapes=[scratch(holders)],
        compiler_params=params(),
        name="grams",
    )(keys, values)
    totals, terms = pl.pallas_call(
        group_totals,
        out_shape=(
            jax.ShapeDtypeStruct((quarters, ROWS * piece, HD), bf16),
            jax.ShapeDtypeStruct(rows.shape, f32),
        ),
        in_specs=[vmem()],
        out_specs=(vmem(), vmem()),
        scratch_shapes=[scratch(ROWS)],
        compiler_params=params(),
        name="group_totals",
    )(exchange(own))
    totals = lax.all_to_all(
        totals, ("far", "near"), 0, 0, axis_index_groups=far_groups(), tiled=True
    )
    states = pl.pallas_call(
        prefixes,
        out_shape=rows,
        in_specs=[vmem(), vmem()],
        out_specs=vmem(),
        scratch_shapes=[scratch(quarters * ROWS), scratch(holders)],
        compiler_params=params(),
        name="prefixes",
    )(terms, totals)
    partial = pl.pallas_call(
        solve,
        out_shape=jax.ShapeDtypeStruct((spread, tokens, out_weight.shape[1] // spread), bf16),
        in_specs=[smem()] + [vmem()] * 5,
        out_specs=vmem(),
        scratch_shapes=[pltpu.VMEM((tokens, width), bf16), scratch(holders)],
        compiler_params=params(),
        name="solve",
    )(ridges, queries, keys, values, exchange(states), out_weight)
    partial = lax.all_to_all(
        partial, "head", 0, 0, axis_index_groups=[HEAD_ORDER], tiled=True
    )
    total = partial[0].astype(f32)
    for n in range(1, spread):
        total += partial[n].astype(f32)
    return total.astype(bf16)


def solution(mesh):
    split = Mesh(mesh.devices.reshape(ROWS, 4, 4, 2, mesh.shape["head"]), (*SEQ, "head"))
    placed = (P(SEQ, "head"), P(SEQ, "head"), P(SEQ, "head"), P("head"), P("head", None))
    return jax.shard_map(
        shards, mesh=split, in_specs=placed, out_specs=P(SEQ, "head"), check_vma=False
    )
```

```python
import jax
import jax.numpy as jnp
from jax import lax
from jax.experimental import pallas as pl
from jax.experimental.pallas import tpu as pltpu
from jax.sharding import Mesh
from jax.sharding import PartitionSpec as P

HD = 128
SEQ = ("y", "far", "near", "core")
EPS = 1e-06
ROWS = 4
SPARE = 8
Y_ORDER, NEAR_ORDER, CORE_ORDER = (2, 1, 0, 3), (2, 3, 0, 1), (1, 0)
FAR_ORDER, HEAD_ORDER = (2, 0, 3, 1), (2, 3, 1, 0)
MEMBERS = [NEAR_ORDER.index(near) * 2 + CORE_ORDER.index(core) for near in range(4) for core in range(2)]
f32, bf16 = jnp.float32, jnp.bfloat16


def vmem():
    return pl.BlockSpec(memory_space=pltpu.VMEM)


def smem():
    return pl.BlockSpec(memory_space=pltpu.SMEM)


def params():
    return pltpu.CompilerParams(vmem_limit_bytes=32 * 1024 * 1024)


def far_groups():
    return [[near + 4 * far if far < 2 else (near + 2) % 4 + 4 * far for far in FAR_ORDER] for near in range(4)]


def near_groups():
    return [
        [((y * 4 + far) * 4 + near) * 2 + core for y in Y_ORDER for near in NEAR_ORDER for core in CORE_ORDER]
        for far in range(4)
    ]


def turned(rows, turns):
    size = rows.shape[0] // (2 * turns)
    parts = [rows[n * size : (n + 1) * size] for n in range(2 * turns)]
    upper = lax.axis_index("far") >= 2
    return jnp.concatenate(
        [jnp.where(upper, parts[n ^ 1], parts[n]) for n in range(2 * turns)], axis=0
    )


def position(axis):
    return lax.broadcasted_iota(jnp.int32, (HD, HD), axis)


def halves(value):
    high = value.astype(bf16)
    return high, (value - high.astype(f32)).astype(bf16)


def pack(value):
    return (value * value * (value * jnp.abs(value))).astype(bf16)


def unpack(coded):
    coded = coded.astype(f32)
    root = jnp.sqrt(jnp.sqrt(jnp.abs(coded)))
    return jnp.where(coded < 0.0, -root, root)


def dot(left, right):
    return jnp.dot(left, right, preferred_element_type=f32)


def key_scale(keys):
    keys = keys.astype(f32)
    return lax.rsqrt(jnp.sum(keys * keys, axis=1, keepdims=True) + EPS)


def grams(k_ref, v_ref, out_ref, keys_ref, values_ref, rows_ref):
    heads = k_ref.shape[1] // HD
    keys_ref[...] = k_ref[...]
    values_ref[...] = v_ref[...]
    squares = []
    for h in range(heads):
        cols = slice(h * HD, (h + 1) * HD)
        keys, values = k_ref[:, cols], v_ref[:, cols]
        scale = key_scale(keys)
        kn = keys.astype(f32) * scale
        key_side = jnp.concatenate(halves(kn * scale), axis=1)
        value_side = jnp.concatenate(halves(kn), axis=1)
        key_gram = dot(keys.T, key_side)
        value_gram = dot(values.T, value_side)
        squares.append(key_gram[:, :HD] + key_gram[:, HD:])
        rows_ref[h * HD : (h + 1) * HD] = value_gram[:, :HD] + value_gram[:, HD:]
    tail = (heads + heads // 2) * HD
    rows_ref[tail:] = jnp.zeros((rows_ref.shape[0] - tail, HD), f32)
    for n in range(heads // 2):
        one, other = squares[2 * n], squares[2 * n + 1]
        at = (heads + n) * HD
        rows_ref[at : at + HD] = jnp.where(position(0) <= position(1), one, other)
        rows_ref[tail + n : tail + n + 1] = jnp.sum(
            jnp.where(position(0) == position(1), other, 0.0), axis=0, keepdims=True
        )
    out_ref[...] = pack(turned(rows_ref[...], ROWS))


def group_totals(near_ref, out_ref, terms_ref, total_ref):
    count = near_ref.shape[0]
    terms_ref[:count] = unpack(near_ref[...])
    terms_ref[count:] = jnp.zeros((SPARE, HD), f32)
    piece = out_ref.shape[1] // ROWS
    members = count // out_ref.shape[1]
    for y in range(ROWS):
        at = Y_ORDER.index(y) * members * piece
        total = terms_ref[at : at + piece]
        for member in range(1, members):
            total += terms_ref[at + member * piece : at + (member + 1) * piece]
        total_ref[y * piece : (y + 1) * piece] = total
    total = pack(total_ref[: out_ref.shape[1]])
    for far in range(out_ref.shape[0]):
        out_ref[far] = total


def prefixes(terms_ref, far_ref, out_ref, total_ref, rows_ref):
    mine = lax.axis_index("far")
    quarters, rows = far_ref.shape[:2]
    piece = rows // ROWS
    for far in range(quarters):
        total_ref[far * rows : (far + 1) * rows] = unpack(far_ref[far])
    before = jnp.zeros((piece, HD), f32)
    for y in range(ROWS):
        running = before
        for far in range(quarters):
            at = far * rows + y * piece
            total = total_ref[at : at + piece]
            running += jnp.where(FAR_ORDER[far] < mine, total, 0.0)
            before += total
        for member in MEMBERS:
            at = (Y_ORDER.index(y) * len(MEMBERS) + member) * piece
            rows_ref[at : at + piece] = running
            running += terms_ref[at : at + piece]
    out_ref[...] = pack(rows_ref[: out_ref.shape[0]])


def solve(ridge_ref, q_ref, k_ref, v_ref, state_ref, w_ref, out_ref, mixed_ref, rows_ref):
    tokens, width = q_ref.shape
    heads = range(width // HD)
    cols = [slice(h * HD, (h + 1) * HD) for h in heads]
    causal = lax.broadcasted_iota(jnp.int32, (tokens, tokens), 0) <= lax.broadcasted_iota(
        jnp.int32, (tokens, tokens), 1
    )

    def total(left, right):
        return jnp.sum(left * right, axis=0, keepdims=True)

    def apply(keys, state, vectors, scale, payload):
        left = jnp.concatenate([keys, state[0]], axis=0)
        left = jnp.concatenate([left] * len(vectors), axis=1)
        both = dot(left, jnp.concatenate(vectors, axis=0))
        scores = jnp.where(causal, both[:tokens] * scale, 0.0).astype(bf16)
        return both[tokens:] + dot(state[1], vectors[0]) + dot(payload, scores)

    keys = [k_ref[:, c] for c in cols]
    scales = [key_scale(k) for k in keys]
    squares = [s * s for s in scales]
    raw = [q_ref[:, c].T for c in cols]
    keys_t = [k.T for k in keys]
    values_t = [v_ref[:, c].T for c in cols]
    rows_ref[...] = turned(unpack(state_ref[...]), ROWS)
    upper, diagonal = position(0) <= position(1), position(0) == position(1)
    tail = (len(heads) + len(heads) // 2) * HD
    states = []
    for n in range(len(heads) // 2):
        at = (len(heads) + n) * HD
        both = rows_ref[at : at + HD]
        mirrored = both.T
        states.append(halves(jnp.where(upper, both, mirrored)))
        other = jnp.where(upper, mirrored, both)
        states.append(halves(jnp.where(diagonal, rows_ref[tail + n : tail + n + 1], other)))
    floats = [r.astype(f32) for r in raw]
    q_scales = [lax.rsqrt(total(f, f) + EPS) for f in floats]
    first = [f * s for f, s in zip(floats, q_scales)]
    norms = [total(d, d) for d in first]
    applied = [
        apply(keys[h], states[h], (raw[h],), squares[h], keys_t[h]) * q_scales[h]
        + ridge_ref[h] * first[h]
        for h in heads
    ]
    steps = [norms[h] / (total(first[h], applied[h]) + EPS) for h in heads]
    residuals = [first[h] - steps[h] * applied[h] for h in heads]
    fresh = [total(r, r) for r in residuals]
    second = [residuals[h] + fresh[h] / (norms[h] + EPS) * first[h] for h in heads]
    applied = [
        apply(keys[h], states[h], halves(second[h]), squares[h], keys_t[h])
        + ridge_ref[h] * second[h]
        for h in heads
    ]
    last = [fresh[h] / (total(second[h], applied[h]) + EPS) for h in heads]
    estimates = [steps[h] * first[h] + last[h] * second[h] for h in heads]
    states = [halves(rows_ref[h * HD : (h + 1) * HD]) for h in heads]
    mixed = [
        apply(keys[h], states[h], halves(estimates[h]), scales[h], values_t[h]) for h in heads
    ]
    for h in heads:
        mixed_ref[:, cols[h]] = mixed[h].T.astype(bf16)
    mixed = mixed_ref[...]
    piece = out_ref.shape[2]
    for n in range(out_ref.shape[0]):
        at = HEAD_ORDER[n] * piece
        out_ref[n] = dot(mixed, w_ref[:, at : at + piece]).astype(bf16)


def shards(queries, keys, values, ridges, out_weight):
    heads = ridges.shape[0]
    tokens, width = queries.shape
    spread, quarters = lax.axis_size("head"), lax.axis_size("far")
    holders = ROWS * lax.axis_size("near") * lax.axis_size("core")
    piece = 2 * pl.cdiv((heads + heads // 2) * HD + heads // 2, 2 * holders)

    def exchange(rows):
        rows = rows.reshape(holders, piece // 2, 2, HD)
        rows = lax.all_to_all(rows, SEQ, 0, 0, axis_index_groups=near_groups(), tiled=True)
        return rows.reshape(holders * piece, HD)

    def scratch(count, spare=0):
        return pltpu.VMEM((count * piece + spare, HD), f32)

    rows = jax.ShapeDtypeStruct((holders * piece, HD), bf16)
    held = jax.ShapeDtypeStruct((tokens, width), bf16)
    own, keys, values = pl.pallas_call(
        grams,
        out_shape=(rows, held, held),
        in_specs=[vmem()] * 2,
        out_specs=(vmem(),) * 3,
        scratch_shapes=[scratch(holders)],
        compiler_params=params(),
        name="grams",
    )(keys, values)
    totals, terms = pl.pallas_call(
        group_totals,
        out_shape=(
            jax.ShapeDtypeStruct((quarters, ROWS * piece, HD), bf16),
            jax.ShapeDtypeStruct((holders * piece + SPARE, HD), f32),
        ),
        in_specs=[vmem()],
        out_specs=(vmem(), vmem()),
        scratch_shapes=[scratch(ROWS, SPARE)],
        compiler_params=params(),
        name="group_totals",
    )(exchange(own))
    totals = lax.all_to_all(
        totals, ("far", "near"), 0, 0, axis_index_groups=far_groups(), tiled=True
    )
    states = pl.pallas_call(
        prefixes,
        out_shape=rows,
        in_specs=[vmem(), vmem()],
        out_specs=vmem(),
        scratch_shapes=[scratch(quarters * ROWS, SPARE), scratch(holders, SPARE)],
        compiler_params=params(),
        name="prefixes",
    )(terms, totals)
    partial = pl.pallas_call(
        solve,
        out_shape=jax.ShapeDtypeStruct((spread, tokens, out_weight.shape[1] // spread), bf16),
        in_specs=[smem()] + [vmem()] * 5,
        out_specs=vmem(),
        scratch_shapes=[pltpu.VMEM((tokens, width), bf16), scratch(holders)],
        compiler_params=params(),
        name="solve",
    )(ridges, queries, keys, values, exchange(states), out_weight)
    partial = lax.all_to_all(
        partial, "head", 0, 0, axis_index_groups=[HEAD_ORDER], tiled=True
    )
    total = partial[0].astype(f32)
    for n in range(1, spread):
        total += partial[n].astype(f32)
    return total.astype(bf16)


def solution(mesh):
    split = Mesh(mesh.devices.reshape(ROWS, 4, 4, 2, mesh.shape["head"]), (*SEQ, "head"))
    placed = (P(SEQ, "head"), P(SEQ, "head"), P(SEQ, "head"), P("head"), P("head", None))
    return jax.shard_map(
        shards, mesh=split, in_specs=placed, out_specs=P(SEQ, "head"), check_vma=False
    )
```
